128 devices in a mesh: ctx: 16 (over y, x_hi, core), head: 8 (over z, x_lo).
Axes of the slice: x: 4 (x_hi: 2, x_lo: 2; x = x_hi * 2 + x_lo), y: 4, z: 4, core: 2. Of those that a mesh axis runs over, the one named last changes fastest.
Arguments:
- queries: bfloat16 [16384, 16384], P(('ctx', 'head')), may hold values from -27 to 27
- key_head_array: bfloat16 [16384, 1024], P(('ctx', 'head')), may hold values from -4 to 4
- value_head_array: bfloat16 [16384, 1024], P(('ctx', 'head')), may hold values from -6 to 6
- output_cotangent: bfloat16 [16384, 16384], P(('ctx', 'head')), may hold values from -6 to 6
- doc_ids: int32 [128], replicated, may hold values from 0 to 32, never falling along the last dimension, each value on 1 to 16 neighbouring positions
Outputs:
- attended: bfloat16 [16384, 16384], P(('ctx', 'head'))
- grad_query: bfloat16 [16384, 16384], P(('ctx', 'head'))
- key_gradient: bfloat16 [16384, 1024], P(('ctx', 'head'))
- value_gradient: bfloat16 [16384, 1024], P(('ctx', 'head'))
The draws below stay inside these ranges and needn't reach their ends.
Inputs may be any that keep to these rules, and one draw needn't show every extreme that they name: `doc_ids`: document ids never fall from block to block; each document covers 1 to 16 whole blocks, and one covers exactly 16.
All inputs are finite; a program needn't handle non-finite values.
Results may differ from the reference program's by a relative error of at most 0.0091.
Values may be sent and summed in bfloat16 or wider, within the bound.
A program may use at most 128 MiB of HBM per device.

```python
import math
import jax
import jax.numpy as jnp
import numpy as np
from jax import lax

QUERY_HEADS = 128
KEY_VALUE_HEADS = 8
HEAD_WIDTH = 128
BLOCK_TOKENS = 128
MAXDOC = 16
PACKED_TOKENS = 16384
NB = 128
DOCS = 33


def draw_queries(key, part):
    key = jax.random.fold_in(key, 11)
    return jnp.clip(jax.random.normal(key, (PACKED_TOKENS, QUERY_HEADS * HEAD_WIDTH), jnp.float32), -4.0, 4.0).astype(jnp.bfloat16)


def draw_key_head_array(key, part):
    key = jax.random.fold_in(key, 12)
    return jnp.clip(jax.random.normal(key, (PACKED_TOKENS, KEY_VALUE_HEADS * HEAD_WIDTH), jnp.float32), -4.0, 4.0).astype(jnp.bfloat16)


def levels(stream_key, extent, cuts, least, largest):
    def one(axis_at, blocks):
        steps = jax.random.uniform(jax.random.fold_in(jax.random.fold_in(stream_key, 6), axis_at), (blocks,), jnp.float32, least / len(cuts), largest / len(cuts))
        return jnp.repeat(jnp.exp(steps), extent[axis_at] // blocks).reshape((-1,) + (1,) * (len(extent) - axis_at - 1))

    level = one(*cuts[0])
    for cut in cuts[1:]:
        level = level * one(*cut)
    return level


def length_profile(number_of, total, limit, slope):
    weights = [(1 << 20) // math.isqrt(grade ** slope) + 1 for grade in range(2, number_of + 1)]
    spare, given = total - limit - (number_of - 1), [1] * (number_of - 1)
    while spare > 0:
        candidates = [i for i in range(number_of - 1) if given[i] < limit]
        pool, remaining = sum([weights[i] for i in candidates]), spare
        for i in candidates:
            addition = min(limit - given[i], max(1, remaining * weights[i] // pool), spare)
            given[i] = given[i] + addition
            spare = spare - addition
    return np.array([limit] + given)


def uneven(own_key, amount, total, most, skew):
    if amount == 2:
        one = jax.random.randint(own_key, (), max(1, total - most), min(most, total - 1) + 1)
        return jnp.stack([one, total - one])
    tallies = jnp.asarray(length_profile(amount, total, most, skew), jnp.int32)
    couples = (amount - 1) // 2
    source_of, sink = tallies[1:1 + 2 * couples:2], tallies[2:2 + 2 * couples:2]
    margin = jnp.minimum(source_of - 1, most - sink)
    passed = jax.random.randint(jax.random.fold_in(own_key, 1), (couples,), 0, 1 << 20) % (margin + 1)
    tallies = tallies.at[1:1 + 2 * couples:2].set(source_of - passed).at[2:2 + 2 * couples:2].set(sink + passed)
    return tallies[jax.random.permutation(jax.random.fold_in(own_key, 2), amount)]


def bell_draw(own_key, extent, deviation, limit, split=(), held_as=jnp.bfloat16):
    values = jax.random.normal(own_key, extent, jnp.float32) * deviation
    if len(split) > 0:
        values = levels(own_key, extent, split, -0.22, 0.18) * values
    return jnp.clip(values, min=-limit, max=limit).astype(held_as)


def setup_inputs(seed: int = 0) -> dict:
    seeds = jax.random.split(jax.random.key(seed), 6)
    return {
        "queries": draw_queries(jax.random.fold_in(seeds[5], 71), 0),
        "key_head_array": draw_key_head_array(jax.random.fold_in(seeds[5], 71), 0),
        "value_head_array": bell_draw(seeds[2], (PACKED_TOKENS, KEY_VALUE_HEADS * HEAD_WIDTH), 1.0, 6.0, ((0, 128),)),
        "output_cotangent": bell_draw(seeds[3], (PACKED_TOKENS, QUERY_HEADS * HEAD_WIDTH), 1.0, 6.0, ((0, 128),)),
        "doc_ids": jnp.searchsorted(jnp.cumsum(uneven(seeds[4], DOCS, NB, MAXDOC, 2)), jnp.arange(NB), side="right").astype(jnp.int32),
    }


def reference(queries, key_head_array, value_head_array, output_cotangent, doc_ids):
    query_group = QUERY_HEADS // KEY_VALUE_HEADS
    scale = HEAD_WIDTH ** -0.5
    spare_margin = (MAXDOC - 1) * BLOCK_TOKENS
    window = MAXDOC * BLOCK_TOKENS
    key_padded = jnp.concatenate([jnp.zeros((spare_margin, KEY_VALUE_HEADS * HEAD_WIDTH), jnp.bfloat16), key_head_array], axis=0).reshape(-1, KEY_VALUE_HEADS, HEAD_WIDTH)
    value_padded = jnp.concatenate([jnp.zeros((spare_margin, KEY_VALUE_HEADS * HEAD_WIDTH), jnp.bfloat16), value_head_array], axis=0).reshape(-1, KEY_VALUE_HEADS, HEAD_WIDTH)
    doc_pad = jnp.concatenate([jnp.full((MAXDOC - 1,), -1, jnp.int32), doc_ids.astype(jnp.int32)])

    def step(carry, block):
        key_gradient_total, value_gradient_total = carry
        tile_rows = (block * BLOCK_TOKENS).astype(jnp.int32)
        query_tile = lax.dynamic_slice_in_dim(queries, tile_rows, BLOCK_TOKENS, 0).reshape(BLOCK_TOKENS, KEY_VALUE_HEADS, query_group, HEAD_WIDTH).astype(jnp.float32)
        gradient_tile = lax.dynamic_slice_in_dim(output_cotangent, tile_rows, BLOCK_TOKENS, 0).reshape(BLOCK_TOKENS, KEY_VALUE_HEADS, query_group, HEAD_WIDTH).astype(jnp.float32)
        k_win = lax.dynamic_slice_in_dim(key_padded, tile_rows, window, 0).astype(jnp.float32)
        v_win = lax.dynamic_slice_in_dim(value_padded, tile_rows, window, 0).astype(jnp.float32)
        key_docs = jnp.repeat(lax.dynamic_slice_in_dim(doc_pad, block.astype(jnp.int32), MAXDOC, 0), BLOCK_TOKENS)
        key_pos = tile_rows - spare_margin + jnp.arange(window, dtype=jnp.int32)
        query_pos = tile_rows + jnp.arange(BLOCK_TOKENS, dtype=jnp.int32)
        allowed = (key_docs[None, :] == doc_ids[block]) & (key_pos[None, :] <= query_pos[:, None])
        allowed = allowed[:, None, None, :]
        scores = jnp.einsum("qhgd,khd->qhgk", query_tile, k_win) * scale
        scores = jnp.where(allowed, scores, -1e30)
        peak = jnp.max(scores, axis=-1)
        expo = jnp.exp(scores - peak[..., None])
        totals = jnp.sum(expo, axis=-1)
        weights = lax.optimization_barrier(expo.astype(jnp.bfloat16)).astype(jnp.float32)
        result = jnp.einsum("qhgk,khd->qhgd", weights, v_win) / totals[..., None]
        result_half = result.astype(jnp.bfloat16)
        log_totals = peak + jnp.log(totals)
        delta = jnp.sum(gradient_tile * lax.optimization_barrier(result_half).astype(jnp.float32), axis=-1)
        probs = jnp.exp(scores - log_totals[..., None])
        probs_half = lax.optimization_barrier(probs.astype(jnp.bfloat16)).astype(jnp.float32)
        value_term = jnp.einsum("qhgk,qhgd->khd", probs_half, gradient_tile)
        dprobs = jnp.einsum("qhgd,khd->qhgk", gradient_tile, v_win)
        dscores = lax.optimization_barrier((probs * (dprobs - delta[..., None])).astype(jnp.bfloat16)).astype(jnp.float32)
        query_grad = jnp.einsum("qhgk,khd->qhgd", dscores, k_win) * scale
        key_term = jnp.einsum("qhgk,qhgd->khd", dscores, query_tile) * scale
        key_gradient_total = lax.dynamic_update_slice_in_dim(key_gradient_total, lax.dynamic_slice_in_dim(key_gradient_total, tile_rows, window, 0) + key_term, tile_rows, 0)
        value_gradient_total = lax.dynamic_update_slice_in_dim(value_gradient_total, lax.dynamic_slice_in_dim(value_gradient_total, tile_rows, window, 0) + value_term, tile_rows, 0)
        return (key_gradient_total, value_gradient_total), (result_half.reshape(BLOCK_TOKENS, QUERY_HEADS * HEAD_WIDTH), query_grad.astype(jnp.bfloat16).reshape(BLOCK_TOKENS, QUERY_HEADS * HEAD_WIDTH))

    start_index = (jnp.zeros((spare_margin + PACKED_TOKENS, KEY_VALUE_HEADS, HEAD_WIDTH), jnp.float32), jnp.zeros((spare_margin + PACKED_TOKENS, KEY_VALUE_HEADS, HEAD_WIDTH), jnp.float32))
    (key_gradient_total, value_gradient_total), (outs, query_grads) = lax.scan(step, start_index, jnp.arange(NB, dtype=jnp.int32))
    attended = outs.reshape(PACKED_TOKENS, QUERY_HEADS * HEAD_WIDTH)
    grad_query = query_grads.reshape(PACKED_TOKENS, QUERY_HEADS * HEAD_WIDTH)
    key_gradient = key_gradient_total[spare_margin:].reshape(PACKED_TOKENS, KEY_VALUE_HEADS * HEAD_WIDTH).astype(jnp.bfloat16)
    value_gradient = value_gradient_total[spare_margin:].reshape(PACKED_TOKENS, KEY_VALUE_HEADS * HEAD_WIDTH).astype(jnp.bfloat16)
    return (attended, grad_query, key_gradient, value_gradient)
```

```python
import jax
import jax.numpy as jnp
from jax import lax
from jax.experimental import pallas as pl
from jax.experimental.pallas import tpu as pltpu
from jax.sharding import PartitionSpec as P

D = 128
GRP = 16
SET = 8
CHUNK = 256
HEADS = 4
STEPS = 4
SCALE = D**-0.5
LOG2E = 1.4426950408889634
BIG = 1e30
F32, BF16 = jnp.float32, jnp.bfloat16


def nt(a, b):
    return lax.dot_general(a, b, (((1,), (1,)), ((), ())), preferred_element_type=F32)


def nn(a, b):
    return lax.dot_general(a, b, (((1,), (0,)), ((), ())), preferred_element_type=F32)


def turned(x):
    return jnp.concatenate([x[:, :D].T, x[:, D:].T], axis=1)


MESH = pl.DeviceIdType.MESH
OWN, BESIDE, DOWN, DOWN_X, FAR, FAR_X, UP, UP_X = range(8)


def kernel(
    ids, q_hbm, g_hbm, k_ref, v_ref,
    o_hbm, dq_hbm, dk_out, dv_out,
    kvh, held, grads, sums, returned, swapped, qm, qo, gm, go, om, oo, dqm, dqo,
    kx, vx, kt, vt, s_scr, e_scr, ds_scr, s_scr2, e_scr2, ds_scr2, dk, dv,
    sw_s, sw_r, pv_s, pv_r, ag_s, ag_r, rs_s, rs_r, ow_s, ow_r, bk_s, bk_r,
    in_l, in_s, in_r, out_l, out_s, out_r,
):
    c, h = lax.axis_index("ctx"), lax.axis_index("head")
    core, chips = c % 2, c // 2
    z, x = h // 2, h % 2
    block = chips * 16 + h

    def reach(last):
        count = 0
        for d in range(1, 16):
            at = jnp.maximum(last - d, 0)
            same = jnp.logical_and(ids[at] == ids[last], last - d >= 0)
            count = count + jnp.where(same, 1, 0)
        return count

    lo_b, lo_8 = 15 - reach(block), 23 - reach(block + 8)
    case_a = lo_8 < 16
    later = core == 1
    sel = jnp.where(case_a, 1.0, 0.0).astype(F32)

    partner = (c + 1 - 2 * core, h)
    near = {
        "x": (c, h + 1 - 2 * x),
        "+": (c, (h + 2) % 8),
        "-": (c, (h + 6) % 8),
    }
    after = [(((chips + 1) % 8) * 2 + k, h) for k in range(2)]
    before = [(((chips + 7) % 8) * 2 + k, h) for k in range(2)]

    barrier = pltpu.get_barrier_semaphore()
    others = [partner, near["x"], near["+"], near["-"]] + after + before
    for device in others:
        pl.semaphore_signal(barrier, inc=1, device_id=device, device_id_type=MESH)
    pl.semaphore_wait(barrier, len(others))

    def remote(src, dst, send, recv, device):
        return pltpu.make_async_remote_copy(
            src_ref=src, dst_ref=dst, send_sem=send, recv_sem=recv,
            device_id=device, device_id_type=MESH,
        )

    def columns(head):
        return pl.ds(pl.multiple_of(head * (GRP * D), GRP * D), GRP * D)

    mine, theirs = core * HEADS, (1 - core) * HEADS

    def swap_out(j):
        return remote(kvh.at[theirs + j], held.at[j, 0, 2 + core], sw_s.at[j], sw_r.at[j], partner)

    def swap_in(j):
        return remote(kvh.at[theirs + j], held.at[j, 0, 3 - core], sw_s.at[j], sw_r.at[j], partner)

    def onward_out(j, k):
        return remote(
            kvh.at[k * HEADS + j], held.at[j, 0, core], pv_s.at[k, j], pv_r.at[core, j], after[k]
        )

    def onward_in(j, k):
        return remote(
            kvh.at[k * HEADS + j], held.at[j, 0, k], pv_s.at[k, j], pv_r.at[k, j], after[k]
        )

    def higher(to, source):
        return jnp.where(to % 4 > source % 4, 1, 0)

    def three(to, source):
        return pl.ds(higher(to, source), 3)

    every = pl.ds(0, 4)
    both, k_only, v_only = pl.ds(0, 2), pl.ds(0, 1), pl.ds(1, 1)
    SPREAD = {
        1: (OWN, BESIDE, "x", every, every, both),
        2: (OWN, UP, "+", every, every, both),
        3: (BESIDE, UP_X, "+", three(z + 1, z), three(z, z + 3), both),
        4: (OWN, DOWN, "-", every, every, both),
        5: (BESIDE, DOWN_X, "-", three(z + 3, z), three(z, z + 1), both),
        6: (UP, FAR, "+", three(z + 1, z + 3), three(z, z + 2), k_only),
        7: (DOWN, FAR, "-", three(z + 3, z + 1), three(z, z + 2), v_only),
        8: (FAR, FAR_X, "x", three(z, z + 2), three(z, z + 2), both),
    }
    COLLECT = {
        1: (BESIDE, "x", every, every, both),
        2: (UP, "-", every, every, both),
        3: (UP_X, "-", three(z, z + 3), three(z + 1, z), both),
        4: (DOWN, "+", every, every, both),
        5: (DOWN_X, "+", three(z, z + 1), three(z + 3, z), both),
        6: (FAR, "-", three(z, z + 2), three(z + 1, z + 3), k_only),
        7: (FAR, "+", three(z, z + 2), three(z + 3, z + 1), v_only),
        8: (FAR_X, "x", three(z, z + 2), three(z, z + 2), both),
    }

    def spread(n, j, arriving=False):
        source, to, way, sent, received, part = SPREAD[n]
        groups = received if arriving else sent
        return remote(
            held.at[j, source, groups, part], held.at[j, to, groups, part],
            ag_s.at[n - 1, j], ag_r.at[n - 1, j], near[way],
        )

    def collect(n, j, arriving=False):
        piece, way, sent, received, part = COLLECT[n]
        groups = received if arriving else sent
        return remote(
            grads.at[j, piece, groups, part], sums.at[j, piece, groups, part],
            rs_s.at[n - 1, j], rs_r.at[n - 1, j], near[way],
        )

    def spread_from(j, *numbers):
        for n in numbers:
            spread(n, j).start()

    def spread_to(j, *numbers):
        for n in numbers:
            spread(n, j, True).wait_recv()

    def collect_from(j, *numbers):
        for n in numbers:
            collect(n, j).start()

    def collect_to(j, *numbers):
        for n in numbers:
            collect(n, j, True).wait_recv()

    def owner_out(j, k):
        return remote(grads.at[j, 0, k], returned.at[core, j], ow_s.at[k, j], ow_r.at[core, j], before[k])

    def owner_in(j, k):
        return remote(grads.at[j, 0, k], returned.at[k, j], ow_s.at[k, j], ow_r.at[k, j], before[k])

    def back(j):
        return remote(grads.at[j, 0, 3 - core], swapped.at[j], bk_s.at[j], bk_r.at[j], partner)

    def local_in(j):
        return [
            pltpu.make_async_copy(src.at[:, columns(mine + j)], dst.at[j], in_l.at[n, j])
            for n, (src, dst) in enumerate(((q_hbm, qm), (g_hbm, gm)))
        ]

    def partner_in(j):
        return [
            remote(src.at[:, columns(theirs + j)], dst.at[j], in_s.at[n, j], in_r.at[n, j], partner)
            for n, (src, dst) in enumerate(((q_hbm, qo), (g_hbm, go)))
        ]

    def local_out(j):
        return [
            pltpu.make_async_copy(src.at[j], dst.at[:, columns(mine + j)], out_l.at[n, j])
            for n, (src, dst) in enumerate(((om, o_hbm), (dqm, dq_hbm)))
        ]

    def partner_out(j, head):
        return [
            remote(src.at[j], dst.at[:, columns(head + j)], out_s.at[n, j], out_r.at[n, j], partner)
            for n, (src, dst) in enumerate(((oo, o_hbm), (dqo, dq_hbm)))
        ]

    def enter(j):
        swap_out(j).start()
        for k in range(2):
            onward_out(j, k).start()

    def entered(j):
        swap_in(j).wait_recv()
        for k in range(2):
            onward_in(j, k).wait_recv()

    for j in range(2 * HEADS):
        kvh[j, 0] = k_ref[:, j * D : (j + 1) * D]
        kvh[j, 1] = v_ref[:, j * D : (j + 1) * D]
    enter(0)
    for copy in partner_in(0) + local_in(0):
        copy.start()
    for j in range(HEADS):
        held[j, 0, 2 + core] = kvh[mine + j]
    entered(0)
    spread_from(0, 1, 2, 4)
    for copy in partner_in(1) + local_in(1):
        copy.start()
    enter(1)

    def clear(j, carry):
        for u in range(8):
            group, piece = place(24 + u)
            grads[j, piece, group] = jnp.zeros((2, D, D), BF16)
        return carry

    def place(w):
        t = (w + h + 1) % 32
        other = t % 8
        return t // 8, 2 * ((other // 2 + 4 - z) % 4) + (other + x) % 2

    lax.fori_loop(0, HEADS, clear, 0)
    spread_to(0, 1)
    spread_from(0, 3, 5)
    spread_to(0, 2, 4)
    spread_from(0, 6, 7)
    for j in range(2, HEADS):
        for copy in partner_in(j) + local_in(j):
            copy.start()
    spread_to(0, 6, 7)
    spread_from(0, 8)
    entered(1)
    spread_from(1, 1, 2, 4)

    starts = (16, 8, jnp.where(case_a, 8, 0))
    lows = (lo_8, lo_b, jnp.where(case_a, lo_8, lo_b))
    sets = (2, 1, jnp.where(case_a, 1, 0))

    def begin(j):
        for copy in local_in(j):
            copy.wait()
        for copy in partner_in(j):
            copy.wait_recv()
        spread_to(j, 3, 5, 8)
        for w in range(3 * SET):
            group, piece = place(w)
            row = pl.ds(w % SET * D, D)
            kb, vb = held[j, piece, group, 0], held[j, piece, group, 1]
            kx[w // SET, row, :] = kb
            vx[w // SET, row, :] = vb
            kt[w // SET, :, row] = kb.T
            vt[w // SET, :, row] = vb.T
        dk[...] = jnp.zeros_like(dk)
        dv[...] = jnp.zeros_like(dv)

    def finish(j):
        for copy in local_out(j) + partner_out(j, mine):
            copy.start()
        for w in range(SET):
            row = pl.ds(w * D, D)
            for n, acc, f in ((0, dk, SCALE), (1, dv, 1.0)):
                for start, value in (
                    (16, acc[0, row, :]),
                    (8, acc[1, row, :] + acc[2, row, :] * sel),
                    (0, acc[2, row, :] * (1.0 - sel)),
                ):
                    group, piece = place(start + w)
                    grads[j, piece, group, n] = (value * f).astype(BF16)
        collect_from(j, 8, 3, 5)

    def add(j, piece, source, groups, count, parts):
        for g in range(count):
            for n in parts:
                total = grads[j, piece, groups.start + g, n].astype(F32)
                for p in source:
                    total = total + sums[j, p, groups.start + g, n].astype(F32)
                grads[j, piece, groups.start + g, n] = total.astype(BF16)

    def collect_far_x(j):
        collect_to(j, 8)
        add(j, FAR, (FAR_X,), COLLECT[8][3], 3, (0, 1))
        collect_from(j, 6, 7)

    def collect_beside(j):
        collect_to(j, 3, 5)
        add(j, BESIDE, (UP_X,), COLLECT[3][3], 3, (0, 1))
        add(j, BESIDE, (DOWN_X,), COLLECT[5][3], 3, (0, 1))
        collect_from(j, 1)

    def collect_far(j):
        collect_to(j, 6, 7)
        add(j, UP, (FAR,), COLLECT[6][3], 3, (0,))
        add(j, DOWN, (FAR,), COLLECT[7][3], 3, (1,))
        collect_from(j, 2, 4)

    def collect_own(j):
        collect_to(j, 1, 2, 4)
        add(j, OWN, (UP, DOWN, BESIDE), every, 4, (0, 1))
        for k in range(2):
            owner_out(j, k).start()
        back(j).start()

    def phases(j, i, s_scr, e_scr, ds_scr):
        lane = pl.ds(pl.multiple_of(i * 2 * D, 2 * D), 2 * D)

        def both(own, other):
            a, b = own[j, :, lane], other[j, :, lane]
            return jnp.where(later, a, b), jnp.where(later, b, a)

        q1, q2 = (jnp.concatenate([a[:, :D], a[:, D:]], axis=0) for a in both(qm, qo))
        g1, g2 = both(gm, go)
        qs = (q1, q2, jnp.where(case_a, q1, q2))
        ms = []
        for t in range(3):
            m = jnp.full((8, 2 * D), -BIG, F32)
            for c in range(4):
                s = nt(kx[sets[t], pl.ds(c * CHUNK, CHUNK), :], qs[t])
                if t < 2 and c == 3:
                    kpos = lax.broadcasted_iota(jnp.int32, (D, 2 * D), 0)
                    qpos = lax.broadcasted_iota(jnp.int32, (D, 2 * D), 1) % D
                    s = jnp.concatenate([s[:D], jnp.where(kpos <= qpos, s[D:], -BIG)], axis=0)
                s_scr[t, pl.ds(c * CHUNK, CHUNK), :] = s
                for b in range(2):
                    bias = jnp.where(starts[t] + 2 * c + b >= lows[t], 0.0, -BIG)
                    part = jnp.max(s[b * D : (b + 1) * D].reshape(16, 8, 2 * D), axis=0)
                    m = jnp.maximum(m, part + bias)
            ms.append(jnp.max(m, axis=0, keepdims=True))
            yield
        m1 = jnp.where(case_a, jnp.maximum(ms[0], ms[2]), ms[0])
        m2 = jnp.where(case_a, ms[1], jnp.maximum(ms[1], ms[2]))
        peaks = (m1, m2, jnp.where(case_a, m1, m2))
        sums, outs = [], []
        factor = SCALE * LOG2E
        for t in range(3):
            l = jnp.zeros((8, 2 * D), F32)
            for c in range(4):
                es = []
                for b in range(2):
                    bias = jnp.where(starts[t] + 2 * c + b >= lows[t], 0.0, BIG)
                    e = jnp.exp2(
                        s_scr[t, pl.ds(c * CHUNK + b * D, D), :] * factor - (peaks[t] * factor + bias)
                    )
                    l = l + jnp.sum(e.reshape(16, 8, 2 * D), axis=0)
                    es.append(e.astype(BF16))
                e_scr[t, pl.ds(c * CHUNK, CHUNK), :] = jnp.concatenate(es, axis=0)
            sums.append(jnp.sum(l, axis=0, keepdims=True))
            outs.append(nn(vt[sets[t]], e_scr[t]))
            yield
        l1 = sums[0] + sums[2] * sel
        l2 = sums[1] + sums[2] * (1.0 - sel)
        o1 = outs[0] + outs[2] * sel
        o2 = outs[1] + outs[2] * (1.0 - sel)
        gs, gts, deltas, results = [], [], [], []
        for g, o, l in ((g1, o1, l1), (g2, o2, l2)):
            inv = 1.0 / l
            half = (o * inv).astype(BF16)
            g32 = turned(g).astype(F32)
            deltas.append(jnp.sum(g32 * half.astype(F32), axis=0, keepdims=True) * inv)
            scaled = (g32 * inv).astype(BF16)
            gts.append(scaled)
            gs.append(jnp.concatenate([scaled[:, :D].T, scaled[:, D:].T], axis=0))
            results.append(turned(half))
        om[j, :, lane] = jnp.where(later, results[0], results[1])
        oo[j, :, lane] = jnp.where(later, results[1], results[0])
        gs.append(jnp.where(case_a, gs[0], gs[1]))
        gts.append(jnp.where(case_a, gts[0], gts[1]))
        deltas.append(jnp.where(case_a, deltas[0], deltas[1]))
        yield
        dqs = []
        for t in range(3):
            for c in range(2):
                row = pl.ds(c * 2 * CHUNK, 2 * CHUNK)
                dp = nn(vx[sets[t], row, :], gts[t])
                ds_scr[row, :] = (dp - deltas[t]).astype(BF16) * e_scr[t, row, :]
            for c in range(2):
                row = pl.ds(c * 2 * CHUNK, 2 * CHUNK)
                dv[t, row, :] += nn(e_scr[t, row, :], gs[t])
                dk[t, row, :] += nn(ds_scr[row, :], qs[t])
            dqs.append(nn(kt[sets[t]], ds_scr[...]))
            yield
        r1 = turned(((dqs[0] + dqs[2] * sel) * SCALE).astype(BF16))
        r2 = turned(((dqs[1] + dqs[2] * (1.0 - sel)) * SCALE).astype(BF16))
        dqm[j, :, lane] = jnp.where(later, r1, r2)
        dqo[j, :, lane] = jnp.where(later, r2, r1)
        yield

    def two_pairs(j, i):
        first = phases(j, 2 * i, s_scr, e_scr, ds_scr)
        second = phases(j, 2 * i + 1, s_scr2, e_scr2, ds_scr2)
        for _ in range(3):
            next(first)
        for _ in range(2):
            for _ in range(3):
                next(first)
                next(second)
            next(first)
        for _ in range(5):
            next(second)

    def step(t, carry):
        j, i = t // STEPS, t % STEPS

        @pl.when(i == 0)
        def _():
            begin(j)

            @pl.when(j < HEADS - 2)
            def _():
                enter(j + 2)

        two_pairs(j, i)

        def service(at, condition, function):
            pl.when(jnp.logical_and(i == at, condition))(function)

        def spread_more():
            spread_to(j + 1, 1)
            spread_from(j + 1, 3, 5)
            spread_to(j + 1, 2, 4)
            spread_from(j + 1, 6, 7)

        def spread_last():
            spread_to(j + 1, 6, 7)
            spread_from(j + 1, 8)

        def spread_first():
            entered(j + 2)
            spread_from(j + 2, 1, 2, 4)

        def collect_first():
            collect_far_x(j - 1)
            collect_beside(j - 1)

        service(0, j < HEADS - 1, spread_more)
        service(0, j > 0, collect_first)
        service(1, j < HEADS - 1, spread_last)
        service(1, j > 0, lambda: collect_far(j - 1))
        service(2, j < HEADS - 2, spread_first)
        service(2, j > 0, lambda: collect_own(j - 1))

        @pl.when(i == STEPS - 1)
        def _():
            finish(j)

        return carry

    lax.fori_loop(0, HEADS * STEPS, step, 0)
    collect_far_x(HEADS - 1)
    collect_beside(HEADS - 1)
    collect_far(HEADS - 1)
    collect_own(HEADS - 1)

    for j in range(HEADS):
        back(j).wait_recv()
        for k in range(2):
            owner_in(j, k).wait_recv()
        for n, out in ((0, dk_out), (1, dv_out)):
            own = grads[j, 0, 2 + core, n].astype(F32)
            other = swapped[j, n].astype(F32)
            first, second = returned[0, j, n].astype(F32), returned[1, j, n].astype(F32)
            low = jnp.where(later, other, own) + first
            high = jnp.where(later, own, other) + second
            out[:, j * D : (j + 1) * D] = low.astype(BF16)
            out[:, (HEADS + j) * D : (HEADS + j + 1) * D] = high.astype(BF16)

    def drain(j, carry):
        swap_out(j).wait_send()
        back(j).wait_send()
        for k in range(2):
            onward_out(j, k).wait_send()
            owner_out(j, k).wait_send()
        for n in range(1, 9):
            spread(n, j).wait_send()
            collect(n, j).wait_send()
        for copy in partner_in(j):
            copy.wait_send()
        for copy in local_out(j):
            copy.wait()
        for copy in partner_out(j, mine):
            copy.wait_send()
        for copy in partner_out(j, theirs):
            copy.wait_recv()
        return carry

    lax.fori_loop(0, HEADS, drain, 0)


def attend(ids, queries, cotangent, keys, values):
    shape = jax.ShapeDtypeStruct
    anywhere, vmem = pl.BlockSpec(memory_space=pl.ANY), pl.BlockSpec(memory_space=pltpu.VMEM)
    blocks = pltpu.VMEM((HEADS, 8, 4, 2, D, D), BF16)
    wide = pltpu.VMEM((HEADS, D, GRP * D), BF16)
    sem = pltpu.SemaphoreType.DMA
    return pl.pallas_call(
        kernel,
        in_specs=[pl.BlockSpec(memory_space=pltpu.SMEM), anywhere, anywhere, vmem, vmem],
        out_specs=[anywhere, anywhere, vmem, vmem],
        out_shape=[shape(queries.shape, BF16)] * 2 + [shape(keys.shape, BF16)] * 2,
        scratch_shapes=[
            pltpu.VMEM((2 * HEADS, 2, D, D), BF16),
            blocks,
            blocks,
            blocks,
            pltpu.VMEM((2, HEADS, 2, D, D), BF16),
            pltpu.VMEM((HEADS, 2, D, D), BF16),
        ]
        + [wide] * 8
        + [
            pltpu.VMEM((3, SET * D, D), BF16),
            pltpu.VMEM((3, SET * D, D), BF16),
            pltpu.VMEM((3, D, SET * D), BF16),
            pltpu.VMEM((3, D, SET * D), BF16),
            pltpu.VMEM((3, SET * D, 2 * D), F32),
            pltpu.VMEM((3, SET * D, 2 * D), BF16),
            pltpu.VMEM((SET * D, 2 * D), BF16),
            pltpu.VMEM((3, SET * D, 2 * D), F32),
            pltpu.VMEM((3, SET * D, 2 * D), BF16),
            pltpu.VMEM((SET * D, 2 * D), BF16),
            pltpu.VMEM((3, SET * D, D), F32),
            pltpu.VMEM((3, SET * D, D), F32),
        ]
        + [sem((HEADS,))] * 2
        + [sem((2, HEADS))] * 2
        + [sem((8, HEADS))] * 4
        + [sem((2, HEADS))] * 2
        + [sem((HEADS,))] * 2
        + [sem((2, HEADS))] * 6,
        compiler_params=pltpu.CompilerParams(
            collective_id=0, has_side_effects=True, vmem_limit_bytes=62 * 1024 * 1024
        ),
        cost_estimate=pl.CostEstimate(
            flops=HEADS * 24 * GRP * 24 * D**3, bytes_accessed=16 * 1024 * 1024, transcendentals=0
        ),
    )(ids, queries, cotangent, keys, values)


def body(queries, keys, values, cotangent, doc_ids):
    attended, grad_query, key_gradient, value_gradient = attend(
        doc_ids, queries, cotangent, keys, values
    )
    return attended, grad_query, key_gradient, value_gradient


def solution(mesh):
    rows = P(("ctx", "head"), None)
    return jax.shard_map(
        body,
        mesh=mesh,
        in_specs=(rows, rows, rows, rows, P()),
        out_specs=(rows, rows, rows, rows),
        check_vma=False,
    )
```

```python
import jax
import jax.numpy as jnp
from jax import lax
from jax.experimental import pallas as pl
from jax.experimental.pallas import tpu as pltpu
from jax.sharding import PartitionSpec as P

D = 128
GRP = 16
SET = 8
CHUNK = 256
HEADS = 4
STEPS = 4
SCALE = D**-0.5
LOG2E = 1.4426950408889634
BIG = 1e30
F32, BF16 = jnp.float32, jnp.bfloat16


def nt(a, b):
    return lax.dot_general(a, b, (((1,), (1,)), ((), ())), preferred_element_type=F32)


def nn(a, b):
    return lax.dot_general(a, b, (((1,), (0,)), ((), ())), preferred_element_type=F32)


def turned(x):
    return jnp.concatenate([x[:, :D].T, x[:, D:].T], axis=1)


MESH = pl.DeviceIdType.MESH
OWN, BESIDE, DOWN, DOWN_X, FAR, FAR_X, UP, UP_X = range(8)


def kernel(
    ids, q_hbm, g_hbm, k_ref, v_ref,
    o_hbm, dq_hbm, dk_out, dv_out,
    kvh, held, grads, sums, returned, swapped, qm, qo, gm, go, om, oo, dqm, dqo,
    kx, vx, kt, vt, s_scr, e_scr, ds_scr, s_scr2, e_scr2, ds_scr2, dk, dv,
    sw_s, sw_r, pv_s, pv_r, ag_s, ag_r, rs_s, rs_r, ow_s, ow_r, bk_s, bk_r,
    in_l, in_s, in_r, out_l, out_s, out_r,
):
    c, h = lax.axis_index("ctx"), lax.axis_index("head")
    core, chips = c % 2, c // 2
    z, x = h // 2, h % 2
    block = chips * 16 + h

    def reach(last):
        count = 0
        for d in range(1, 16):
            at = jnp.maximum(last - d, 0)
            same = jnp.logical_and(ids[at] == ids[last], last - d >= 0)
            count = count + jnp.where(same, 1, 0)
        return count

    lo_b, lo_8 = 15 - reach(block), 23 - reach(block + 8)
    case_a = lo_8 < 16
    later = core == 1
    sel = jnp.where(case_a, 1.0, 0.0).astype(F32)

    partner = (c + 1 - 2 * core, h)
    near = {
        "x": (c, h + 1 - 2 * x),
        "+": (c, (h + 2) % 8),
        "-": (c, (h + 6) % 8),
    }
    after = [(((chips + 1) % 8) * 2 + k, h) for k in range(2)]
    before = [(((chips + 7) % 8) * 2 + k, h) for k in range(2)]

    barrier = pltpu.get_barrier_semaphore()
    others = [partner, near["x"], near["+"], near["-"]] + after + before
    for device in others:
        pl.semaphore_signal(barrier, inc=1, device_id=device, device_id_type=MESH)
    def remote(src, dst, send, recv, device):
        return pltpu.make_async_remote_copy(
            src_ref=src, dst_ref=dst, send_sem=send, recv_sem=recv,
            device_id=device, device_id_type=MESH,
        )

    def columns(head):
        return pl.ds(pl.multiple_of(head * (GRP * D), GRP * D), GRP * D)

    mine, theirs = core * HEADS, (1 - core) * HEADS

    def swap_out(j):
        return remote(kvh.at[theirs + j], held.at[j, 0, 2 + core], sw_s.at[j], sw_r.at[j], partner)

    def swap_in(j):
        return remote(kvh.at[theirs + j], held.at[j, 0, 3 - core], sw_s.at[j], sw_r.at[j], partner)

    def onward_out(j, k):
        return remote(
            kvh.at[k * HEADS + j], held.at[j, 0, core], pv_s.at[k, j], pv_r.at[core, j], after[k]
        )

    def onward_in(j, k):
        return remote(
            kvh.at[k * HEADS + j], held.at[j, 0, k], pv_s.at[k, j], pv_r.at[k, j], after[k]
        )

    def higher(to, source):
        return jnp.where(to % 4 > source % 4, 1, 0)

    def three(to, source):
        return pl.ds(higher(to, source), 3)

    every, old, new = pl.ds(0, 4), pl.ds(0, 2), pl.ds(2, 2)
    both, k_only, v_only = pl.ds(0, 2), pl.ds(0, 1), pl.ds(1, 1)
    SPREAD = {
        1: (OWN, BESIDE, "x", old, old, both),
        2: (OWN, UP, "+", old, old, both),
        3: (BESIDE, UP_X, "+", three(z + 1, z), three(z, z + 3), both),
        4: (OWN, DOWN, "-", old, old, both),
        5: (BESIDE, DOWN_X, "-", three(z + 3, z), three(z, z + 1), both),
        6: (UP, FAR, "+", three(z + 1, z + 3), three(z, z + 2), k_only),
        7: (DOWN, FAR, "-", three(z + 3, z + 1), three(z, z + 2), v_only),
        8: (FAR, FAR_X, "x", three(z, z + 2), three(z, z + 2), both),
        9: (OWN, BESIDE, "x", new, new, both),
        10: (OWN, UP, "+", new, new, both),
        11: (OWN, DOWN, "-", new, new, both),
    }
    COLLECT = {
        1: (BESIDE, "x", every, every, both),
        2: (UP, "-", every, every, k_only),
        3: (UP_X, "-", three(z, z + 3), three(z + 1, z), both),
        4: (DOWN, "+", every, every, v_only),
        5: (DOWN_X, "+", three(z, z + 1), three(z + 3, z), both),
        6: (FAR, "-", three(z, z + 2), three(z + 1, z + 3), k_only),
        7: (FAR, "+", three(z, z + 2), three(z + 3, z + 1), v_only),
        8: (FAR_X, "x", three(z, z + 2), three(z, z + 2), both),
        9: (UP, "-", every, every, v_only),
        10: (DOWN, "+", every, every, k_only),
    }

    def spread(n, j, arriving=False):
        source, to, way, sent, received, part = SPREAD[n]
        groups = received if arriving else sent
        return remote(
            held.at[j, source, groups, part], held.at[j, to, groups, part],
            ag_s.at[n - 1, j], ag_r.at[n - 1, j], near[way],
        )

    def collect(n, j, arriving=False):
        piece, way, sent, received, part = COLLECT[n]
        groups = received if arriving else sent
        return remote(
            grads.at[j, piece, groups, part], sums.at[j, piece, groups, part],
            rs_s.at[n - 1, j], rs_r.at[n - 1, j], near[way],
        )

    def spread_from(j, *numbers):
        for n in numbers:
            spread(n, j).start()

    def first_spread(j):
        entered_new(j)
        spread_from(j, 10, 11, 9)
        entered_old(j)
        spread_from(j, 2, 4, 1)

    def spread_to(j, *numbers):
        for n in numbers:
            spread(n, j, True).wait_recv()

    def collect_from(j, *numbers):
        for n in numbers:
            collect(n, j).start()

    def collect_to(j, *numbers):
        for n in numbers:
            collect(n, j, True).wait_recv()

    def owner_out(j, k):
        return remote(grads.at[j, 0, k], returned.at[core, j], ow_s.at[k, j], ow_r.at[core, j], before[k])

    def owner_in(j, k):
        return remote(grads.at[j, 0, k], returned.at[k, j], ow_s.at[k, j], ow_r.at[k, j], before[k])

    def back(j):
        return remote(grads.at[j, 0, 3 - core], swapped.at[j], bk_s.at[j], bk_r.at[j], partner)

    def local_in(j):
        return [
            pltpu.make_async_copy(src.at[:, columns(mine + j)], dst.at[j], in_l.at[n, j])
            for n, (src, dst) in enumerate(((q_hbm, qm), (g_hbm, gm)))
        ]

    def partner_in(j):
        return [
            remote(src.at[:, columns(theirs + j)], dst.at[j], in_s.at[n, j], in_r.at[n, j], partner)
            for n, (src, dst) in enumerate(((q_hbm, qo), (g_hbm, go)))
        ]

    def local_out(j):
        return [
            pltpu.make_async_copy(src.at[j], dst.at[:, columns(mine + j)], out_l.at[n, j])
            for n, (src, dst) in enumerate(((om, o_hbm), (dqm, dq_hbm)))
        ]

    def partner_out(j, head):
        return [
            remote(src.at[j], dst.at[:, columns(head + j)], out_s.at[n, j], out_r.at[n, j], partner)
            for n, (src, dst) in enumerate(((oo, o_hbm), (dqo, dq_hbm)))
        ]

    def enter(j):
        swap_out(j).start()
        for k in range(2):
            onward_out(j, k).start()

    def entered_new(j):
        swap_in(j).wait_recv()

    def entered_old(j):
        for k in range(2):
            onward_in(j, k).wait_recv()

    for copy in local_in(0):
        copy.start()
    for j in range(2 * HEADS):
        kvh[j, 0] = k_ref[:, j * D : (j + 1) * D]
        kvh[j, 1] = v_ref[:, j * D : (j + 1) * D]
    for j in range(HEADS):
        held[j, 0, 2 + core] = kvh[mine + j]
    pl.semaphore_wait(barrier, len(others))
    enter(0)
    entered_new(0)
    spread_from(0, 10, 11, 9)
    for copy in partner_in(0):
        copy.start()
    entered_old(0)
    spread_from(0, 2, 4, 1)
    enter(1)
    for copy in partner_in(1) + local_in(1):
        copy.start()

    def clear(j, carry):
        for u in range(8):
            group, piece = place(24 + u)
            grads[j, piece, group] = jnp.zeros((2, D, D), BF16)
        return carry

    def place(w):
        t = (w + h + 1) % 32
        other = t % 8
        return t // 8, 2 * ((other // 2 + 4 - z) % 4) + (other + x) % 2

    lax.fori_loop(0, HEADS, clear, 0)
    spread_to(0, 10, 11, 2, 4)
    spread_from(0, 6, 7)
    spread_to(0, 9, 1)
    spread_from(0, 3, 5)
    for j in range(2, HEADS):
        for copy in partner_in(j) + local_in(j):
            copy.start()
    spread_to(0, 6, 7)
    spread_from(0, 8)
    first_spread(1)

    starts = (16, 8, jnp.where(case_a, 8, 0))
    lows = (lo_8, lo_b, jnp.where(case_a, lo_8, lo_b))
    sets = (2, 1, jnp.where(case_a, 1, 0))

    def begin(j):
        for copy in local_in(j):
            copy.wait()
        for copy in partner_in(j):
            copy.wait_recv()
        spread_to(j, 3, 5, 8)
        for w in range(3 * SET):
            group, piece = place(w)
            row = pl.ds(w % SET * D, D)
            kb, vb = held[j, piece, group, 0], held[j, piece, group, 1]
            kx[w // SET, row, :] = kb
            vx[w // SET, row, :] = vb
            kt[w // SET, :, row] = kb.T
            vt[w // SET, :, row] = vb.T
        dk[...] = jnp.zeros_like(dk)
        dv[...] = jnp.zeros_like(dv)

    def finish(j):
        for copy in local_out(j) + partner_out(j, mine):
            copy.start()
        for w in range(SET):
            row = pl.ds(w * D, D)
            for n, acc, f in ((0, dk, SCALE), (1, dv, 1.0)):
                for start, value in (
                    (16, acc[0, row, :]),
                    (8, acc[1, row, :] + acc[2, row, :] * sel),
                    (0, acc[2, row, :] * (1.0 - sel)),
                ):
                    group, piece = place(start + w)
                    grads[j, piece, group, n] = (value * f).astype(BF16)
        collect_from(j, 8, 3, 5, 9, 10)

    def add(j, piece, source, groups, count, parts):
        for g in range(count):
            for n in parts:
                total = grads[j, piece, groups.start + g, n].astype(F32)
                for p in source:
                    total = total + sums[j, p, groups.start + g, n].astype(F32)
                grads[j, piece, groups.start + g, n] = total.astype(BF16)

    def collect_far_x(j):
        collect_to(j, 8)
        add(j, FAR, (FAR_X,), COLLECT[8][3], 3, (0, 1))
        collect_from(j, 6, 7)

    def collect_beside(j):
        collect_to(j, 3, 5)
        add(j, BESIDE, (UP_X,), COLLECT[3][3], 3, (0, 1))
        add(j, BESIDE, (DOWN_X,), COLLECT[5][3], 3, (0, 1))
        collect_from(j, 1)

    def collect_far(j):
        collect_to(j, 6, 7)
        add(j, UP, (FAR,), COLLECT[6][3], 3, (0,))
        add(j, DOWN, (FAR,), COLLECT[7][3], 3, (1,))
        collect_from(j, 2, 4)

    def collect_own(j):
        collect_to(j, 1, 2, 4, 9, 10)
        add(j, OWN, (UP, DOWN, BESIDE), every, 4, (0, 1))
        for k in range(2):
            owner_out(j, k).start()
        back(j).start()

    def phases(j, i, s_scr, e_scr, ds_scr):
        lane = pl.ds(pl.multiple_of(i * 2 * D, 2 * D), 2 * D)

        def both(own, other):
            a, b = own[j, :, lane], other[j, :, lane]
            return jnp.where(later, a, b), jnp.where(later, b, a)

        q1, q2 = (jnp.concatenate([a[:, :D], a[:, D:]], axis=0) for a in both(qm, qo))
        g1, g2 = both(gm, go)
        qs = (q1, q2, jnp.where(case_a, q1, q2))
        ms = []
        for t in range(3):
            m = jnp.full((8, 2 * D), -BIG, F32)
            for c in range(4):
                s = nt(kx[sets[t], pl.ds(c * CHUNK, CHUNK), :], qs[t])
                if t < 2 and c == 3:
                    kpos = lax.broadcasted_iota(jnp.int32, (D, 2 * D), 0)
                    qpos = lax.broadcasted_iota(jnp.int32, (D, 2 * D), 1) % D
                    s = jnp.concatenate([s[:D], jnp.where(kpos <= qpos, s[D:], -BIG)], axis=0)
                s_scr[t, pl.ds(c * CHUNK, CHUNK), :] = s
                for b in range(2):
                    bias = jnp.where(starts[t] + 2 * c + b >= lows[t], 0.0, -BIG)
                    part = jnp.max(s[b * D : (b + 1) * D].reshape(16, 8, 2 * D), axis=0)
                    m = jnp.maximum(m, part + bias)
            ms.append(jnp.max(m, axis=0, keepdims=True))
            yield
        m1 = jnp.where(case_a, jnp.maximum(ms[0], ms[2]), ms[0])
        m2 = jnp.where(case_a, ms[1], jnp.maximum(ms[1], ms[2]))
        peaks = (m1, m2, jnp.where(case_a, m1, m2))
        sums, outs = [], []
        factor = SCALE * LOG2E
        for t in range(3):
            l = jnp.zeros((8, 2 * D), F32)
            for c in range(4):
                es = []
                for b in range(2):
                    bias = jnp.where(starts[t] + 2 * c + b >= lows[t], 0.0, BIG)
                    e = jnp.exp2(
                        s_scr[t, pl.ds(c * CHUNK + b * D, D), :] * factor - (peaks[t] * factor + bias)
                    )
                    l = l + jnp.sum(e.reshape(16, 8, 2 * D), axis=0)
                    es.append(e.astype(BF16))
                e_scr[t, pl.ds(c * CHUNK, CHUNK), :] = jnp.concatenate(es, axis=0)
            sums.append(jnp.sum(l, axis=0, keepdims=True))
            outs.append(nn(vt[sets[t]], e_scr[t]))
            yield
        l1 = sums[0] + sums[2] * sel
        l2 = sums[1] + sums[2] * (1.0 - sel)
        o1 = outs[0] + outs[2] * sel
        o2 = outs[1] + outs[2] * (1.0 - sel)
        gs, gts, deltas, results = [], [], [], []
        for g, o, l in ((g1, o1, l1), (g2, o2, l2)):
            inv = 1.0 / l
            half = (o * inv).astype(BF16)
            g32 = turned(g).astype(F32)
            deltas.append(jnp.sum(g32 * half.astype(F32), axis=0, keepdims=True) * inv)
            scaled = (g32 * inv).astype(BF16)
            gts.append(scaled)
            gs.append(jnp.concatenate([scaled[:, :D].T, scaled[:, D:].T], axis=0))
            results.append(turned(half))
        om[j, :, lane] = jnp.where(later, results[0], results[1])
        oo[j, :, lane] = jnp.where(later, results[1], results[0])
        gs.append(jnp.where(case_a, gs[0], gs[1]))
        gts.append(jnp.where(case_a, gts[0], gts[1]))
        deltas.append(jnp.where(case_a, deltas[0], deltas[1]))
        yield
        dqs = []
        for t in range(3):
            for c in range(2):
                row = pl.ds(c * 2 * CHUNK, 2 * CHUNK)
                dp = nn(vx[sets[t], row, :], gts[t])
                ds_scr[row, :] = (dp - deltas[t]).astype(BF16) * e_scr[t, row, :]
            for c in range(2):
                row = pl.ds(c * 2 * CHUNK, 2 * CHUNK)
                dv[t, row, :] += nn(e_scr[t, row, :], gs[t])
                dk[t, row, :] += nn(ds_scr[row, :], qs[t])
            dqs.append(nn(kt[sets[t]], ds_scr[...]))
            yield
        r1 = turned(((dqs[0] + dqs[2] * sel) * SCALE).astype(BF16))
        r2 = turned(((dqs[1] + dqs[2] * (1.0 - sel)) * SCALE).astype(BF16))
        dqm[j, :, lane] = jnp.where(later, r1, r2)
        dqo[j, :, lane] = jnp.where(later, r2, r1)
        yield

    def two_pairs(j, i):
        first = phases(j, 2 * i, s_scr, e_scr, ds_scr)
        second = phases(j, 2 * i + 1, s_scr2, e_scr2, ds_scr2)
        for _ in range(3):
            next(first)
        for _ in range(2):
            for _ in range(3):
                next(first)
                next(second)
            next(first)
        for _ in range(5):
            next(second)

    def step(t, carry):
        j, i = t // STEPS, t % STEPS

        @pl.when(i == 0)
        def _():
            begin(j)

            @pl.when(j < HEADS - 2)
            def _():
                enter(j + 2)

        two_pairs(j, i)

        def service(at, condition, function):
            pl.when(jnp.logical_and(i == at, condition))(function)

        def first_services():
            @pl.when(j < HEADS - 1)
            def _():
                spread_to(j + 1, 10, 11, 2, 4)
                spread_from(j + 1, 6, 7)

            @pl.when(j > 0)
            def _():
                collect_far_x(j - 1)

            @pl.when(j < HEADS - 1)
            def _():
                spread_to(j + 1, 9, 1)
                spread_from(j + 1, 3, 5)

            @pl.when(j > 0)
            def _():
                collect_beside(j - 1)

        def spread_last():
            spread_to(j + 1, 6, 7)
            spread_from(j + 1, 8)

        def spread_first():
            first_spread(j + 2)

        service(0, True, first_services)
        service(1, j < HEADS - 1, spread_last)
        service(1, j > 0, lambda: collect_far(j - 1))
        service(2, j < HEADS - 2, spread_first)
        service(3, j > 0, lambda: collect_own(j - 1))

        @pl.when(i == STEPS - 1)
        def _():
            finish(j)

        return carry

    lax.fori_loop(0, HEADS * STEPS, step, 0)
    def final(j):
        back(j).wait_recv()
        for k in range(2):
            owner_in(j, k).wait_recv()
        for n, out in ((0, dk_out), (1, dv_out)):
            own = grads[j, 0, 2 + core, n].astype(F32)
            other = swapped[j, n].astype(F32)
            first, second = returned[0, j, n].astype(F32), returned[1, j, n].astype(F32)
            low = jnp.where(later, other, own) + first
            high = jnp.where(later, own, other) + second
            out[:, j * D : (j + 1) * D] = low.astype(BF16)
            out[:, (HEADS + j) * D : (HEADS + j + 1) * D] = high.astype(BF16)

    def drain(j, carry):
        swap_out(j).wait_send()
        back(j).wait_send()
        for k in range(2):
            onward_out(j, k).wait_send()
            owner_out(j, k).wait_send()
        for n in range(1, 12):
            spread(n, j).wait_send()
        for n in range(1, 11):
            collect(n, j).wait_send()
        for copy in partner_in(j):
            copy.wait_send()
        for copy in local_out(j):
            copy.wait()
        for copy in partner_out(j, mine):
            copy.wait_send()
        for copy in partner_out(j, theirs):
            copy.wait_recv()
        return carry

    for j in range(HEADS - 1):
        final(j)
    collect_far_x(HEADS - 1)
    collect_beside(HEADS - 1)
    lax.fori_loop(0, HEADS - 1, drain, 0)
    collect_far(HEADS - 1)
    collect_own(HEADS - 1)
    final(HEADS - 1)
    drain(HEADS - 1, 0)


def attend(ids, queries, cotangent, keys, values):
    shape = jax.ShapeDtypeStruct
    anywhere, vmem = pl.BlockSpec(memory_space=pl.ANY), pl.BlockSpec(memory_space=pltpu.VMEM)
    blocks = pltpu.VMEM((HEADS, 8, 4, 2, D, D), BF16)
    wide = pltpu.VMEM((HEADS, D, GRP * D), BF16)
    sem = pltpu.SemaphoreType.DMA
    return pl.pallas_call(
        kernel,
        in_specs=[pl.BlockSpec(memory_space=pltpu.SMEM), anywhere, anywhere, vmem, vmem],
        out_specs=[anywhere, anywhere, vmem, vmem],
        out_shape=[shape(queries.shape, BF16)] * 2 + [shape(keys.shape, BF16)] * 2,
        scratch_shapes=[
            pltpu.VMEM((2 * HEADS, 2, D, D), BF16),
            blocks,
            blocks,
            blocks,
            pltpu.VMEM((2, HEADS, 2, D, D), BF16),
            pltpu.VMEM((HEADS, 2, D, D), BF16),
        ]
        + [wide] * 8
        + [
            pltpu.VMEM((3, SET * D, D), BF16),
            pltpu.VMEM((3, SET * D, D), BF16),
            pltpu.VMEM((3, D, SET * D), BF16),
            pltpu.VMEM((3, D, SET * D), BF16),
            pltpu.VMEM((3, SET * D, 2 * D), F32),
            pltpu.VMEM((3, SET * D, 2 * D), BF16),
            pltpu.VMEM((SET * D, 2 * D), BF16),
            pltpu.VMEM((3, SET * D, 2 * D), F32),
            pltpu.VMEM((3, SET * D, 2 * D), BF16),
            pltpu.VMEM((SET * D, 2 * D), BF16),
            pltpu.VMEM((3, SET * D, D), F32),
            pltpu.VMEM((3, SET * D, D), F32),
        ]
        + [sem((HEADS,))] * 2
        + [sem((2, HEADS))] * 2
        + [sem((11, HEADS))] * 2
        + [sem((10, HEADS))] * 2
        + [sem((2, HEADS))] * 2
        + [sem((HEADS,))] * 2
        + [sem((2, HEADS))] * 6,
        compiler_params=pltpu.CompilerParams(
            collective_id=0, has_side_effects=True, vmem_limit_bytes=62 * 1024 * 1024
        ),
        cost_estimate=pl.CostEstimate(
            flops=HEADS * 24 * GRP * 24 * D**3, bytes_accessed=16 * 1024 * 1024, transcendentals=0
        ),
    )(ids, queries, cotangent, keys, values)


def body(queries, keys, values, cotangent, doc_ids):
    attended, grad_query, key_gradient, value_gradient = attend(
        doc_ids, queries, cotangent, keys, values
    )
    return attended, grad_query, key_gradient, value_gradient


def solution(mesh):
    rows = P(("ctx", "head"), None)
    return jax.shard_map(
        body,
        mesh=mesh,
        in_specs=(rows, rows, rows, rows, P()),
        out_specs=(rows, rows, rows, rows),
        check_vma=False,
    )
```

```python
import jax
import jax.numpy as jnp
from jax import lax
from jax.experimental import pallas as pl
from jax.experimental.pallas import tpu as pltpu
from jax.sharding import PartitionSpec as P

D = 128
GRP = 16
SET = 8
CHUNK = 256
HEADS = 4
STEPS = 4
SCALE = D**-0.5
LOG2E = 1.4426950408889634
BIG = 1e30
F32, BF16 = jnp.float32, jnp.bfloat16


def nt(a, b):
    return lax.dot_general(a, b, (((1,), (1,)), ((), ())), preferred_element_type=F32)


def nn(a, b):
    return lax.dot_general(a, b, (((1,), (0,)), ((), ())), preferred_element_type=F32)


def turned(x):
    return jnp.concatenate([x[:, :D].T, x[:, D:].T], axis=1)


MESH = pl.DeviceIdType.MESH
OWN, BESIDE, DOWN, DOWN_X, FAR, FAR_X, UP, UP_X = range(8)


def kernel(
    ids, q_hbm, g_hbm, k_ref, v_ref,
    o_hbm, dq_hbm, dk_out, dv_out,
    kvh, held, grads, sums, returned, swapped, qm, qo, gm, go, om, oo, dqm, dqo,
    kx, vx, kt, vt, s_scr, e_scr, ds_scr, s_scr2, e_scr2, ds_scr2, dk, dv,
    sw_s, sw_r, pv_s, pv_r, ag_s, ag_r, rs_s, rs_r, ow_s, ow_r, bk_s, bk_r,
    in_l, in_s, in_r, out_l, out_s, out_r,
):
    c, h = lax.axis_index("ctx"), lax.axis_index("head")
    core, chips = c % 2, c // 2
    z, x = h // 2, h % 2
    block = chips * 16 + h

    def reach(last):
        count = 0
        for d in range(1, 16):
            at = jnp.maximum(last - d, 0)
            same = jnp.logical_and(ids[at] == ids[last], last - d >= 0)
            count = count + jnp.where(same, 1, 0)
        return count

    lo_b, lo_8 = 15 - reach(block), 23 - reach(block + 8)
    case_a = lo_8 < 16
    later = core == 1
    sel = jnp.where(case_a, 1.0, 0.0).astype(F32)

    partner = (c + 1 - 2 * core, h)
    near = {
        "x": (c, h + 1 - 2 * x),
        "+": (c, (h + 2) % 8),
        "-": (c, (h + 6) % 8),
    }
    after = [(((chips + 1) % 8) * 2 + k, h) for k in range(2)]
    before = [(((chips + 7) % 8) * 2 + k, h) for k in range(2)]

    barrier = pltpu.get_barrier_semaphore()
    others = [partner, near["x"], near["+"], near["-"]] + after + before
    for device in others:
        pl.semaphore_signal(barrier, inc=1, device_id=device, device_id_type=MESH)
    def remote(src, dst, send, recv, device):
        return pltpu.make_async_remote_copy(
            src_ref=src, dst_ref=dst, send_sem=send, recv_sem=recv,
            device_id=device, device_id_type=MESH,
        )

    def columns(head):
        return pl.ds(pl.multiple_of(head * (GRP * D), GRP * D), GRP * D)

    mine, theirs = core * HEADS, (1 - core) * HEADS

    def swap_out(j):
        return remote(kvh.at[theirs + j], held.at[j, 0, 2 + core], sw_s.at[j], sw_r.at[j], partner)

    def swap_in(j):
        return remote(kvh.at[theirs + j], held.at[j, 0, 3 - core], sw_s.at[j], sw_r.at[j], partner)

    def onward_out(j, k):
        return remote(
            kvh.at[k * HEADS + j], held.at[j, 0, core], pv_s.at[k, j], pv_r.at[core, j], after[k]
        )

    def onward_in(j, k):
        return remote(
            kvh.at[k * HEADS + j], held.at[j, 0, k], pv_s.at[k, j], pv_r.at[k, j], after[k]
        )

    def higher(to, source):
        return jnp.where(to % 4 > source % 4, 1, 0)

    def three(to, source):
        return pl.ds(higher(to, source), 3)

    every, old, new = pl.ds(0, 4), pl.ds(0, 2), pl.ds(2, 2)
    both, k_only, v_only = pl.ds(0, 2), pl.ds(0, 1), pl.ds(1, 1)
    SPREAD = {
        1: (OWN, BESIDE, "x", old, old, both),
        2: (OWN, UP, "+", old, old, both),
        3: (BESIDE, UP_X, "+", three(z + 1, z), three(z, z + 3), both),
        4: (OWN, DOWN, "-", old, old, both),
        5: (BESIDE, DOWN_X, "-", three(z + 3, z), three(z, z + 1), both),
        6: (UP, FAR, "+", three(z + 1, z + 3), three(z, z + 2), k_only),
        7: (DOWN, FAR, "-", three(z + 3, z + 1), three(z, z + 2), v_only),
        8: (FAR, FAR_X, "x", three(z, z + 2), three(z, z + 2), both),
        9: (OWN, BESIDE, "x", new, new, both),
        10: (OWN, UP, "+", new, new, both),
        11: (OWN, DOWN, "-", new, new, both),
    }
    COLLECT = {
        1: (BESIDE, "x", every, every, both),
        2: (UP, "-", every, every, k_only),
        3: (UP_X, "-", three(z, z + 3), three(z + 1, z), both),
        4: (DOWN, "+", every, every, v_only),
        5: (DOWN_X, "+", three(z, z + 1), three(z + 3, z), both),
        6: (FAR, "-", three(z, z + 2), three(z + 1, z + 3), k_only),
        7: (FAR, "+", three(z, z + 2), three(z + 3, z + 1), v_only),
        8: (FAR_X, "x", three(z, z + 2), three(z, z + 2), both),
        9: (UP, "-", every, every, v_only),
        10: (DOWN, "+", every, every, k_only),
    }

    def spread(n, j, arriving=False):
        source, to, way, sent, received, part = SPREAD[n]
        groups = received if arriving else sent
        return remote(
            held.at[j, source, groups, part], held.at[j, to, groups, part],
            ag_s.at[n - 1, j], ag_r.at[n - 1, j], near[way],
        )

    def collect(n, j, arriving=False):
        piece, way, sent, received, part = COLLECT[n]
        groups = received if arriving else sent
        return remote(
            grads.at[j, piece, groups, part], sums.at[j, piece, groups, part],
            rs_s.at[n - 1, j], rs_r.at[n - 1, j], near[way],
        )

    def spread_from(j, *numbers):
        for n in numbers:
            spread(n, j).start()

    def first_spread(j):
        entered_new(j)
        spread_from(j, 10, 11, 9)
        entered_old(j)
        spread_from(j, 2, 4, 1)

    def spread_to(j, *numbers):
        for n in numbers:
            spread(n, j, True).wait_recv()

    def collect_from(j, *numbers):
        for n in numbers:
            collect(n, j).start()

    def collect_to(j, *numbers):
        for n in numbers:
            collect(n, j, True).wait_recv()

    def owner_out(j, k):
        return remote(grads.at[j, 0, k], returned.at[core, j], ow_s.at[k, j], ow_r.at[core, j], before[k])

    def owner_in(j, k):
        return remote(grads.at[j, 0, k], returned.at[k, j], ow_s.at[k, j], ow_r.at[k, j], before[k])

    def back(j):
        return remote(grads.at[j, 0, 3 - core], swapped.at[j], bk_s.at[j], bk_r.at[j], partner)

    def local_in(j):
        return [
            pltpu.make_async_copy(src.at[:, columns(mine + j)], dst.at[j], in_l.at[n, j])
            for n, (src, dst) in enumerate(((q_hbm, qm), (g_hbm, gm)))
        ]

    def partner_in(j):
        return [
            remote(src.at[:, columns(theirs + j)], dst.at[j], in_s.at[n, j], in_r.at[n, j], partner)
            for n, (src, dst) in enumerate(((q_hbm, qo), (g_hbm, go)))
        ]

    def local_out(j):
        return [
            pltpu.make_async_copy(src.at[j], dst.at[:, columns(mine + j)], out_l.at[n, j])
            for n, (src, dst) in enumerate(((om, o_hbm), (dqm, dq_hbm)))
        ]

    def partner_out(j, head):
        return [
            remote(src.at[j], dst.at[:, columns(head + j)], out_s.at[n, j], out_r.at[n, j], partner)
            for n, (src, dst) in enumerate(((oo, o_hbm), (dqo, dq_hbm)))
        ]

    def enter(j):
        swap_out(j).start()
        for k in range(2):
            onward_out(j, k).start()

    def entered_new(j):
        swap_in(j).wait_recv()

    def entered_old(j):
        for k in range(2):
            onward_in(j, k).wait_recv()

    for copy in local_in(0):
        copy.start()
    for j in range(2 * HEADS):
        kvh[j, 0] = k_ref[:, j * D : (j + 1) * D]
        kvh[j, 1] = v_ref[:, j * D : (j + 1) * D]
    for j in range(HEADS):
        held[j, 0, 2 + core] = kvh[mine + j]
    pl.semaphore_wait(barrier, len(others))
    enter(0)
    entered_new(0)
    spread_from(0, 10, 11, 9)
    for copy in partner_in(0):
        copy.start()
    entered_old(0)
    spread_from(0, 2, 4, 1)
    enter(1)
    for copy in partner_in(1) + local_in(1):
        copy.start()

    def clear(j, carry):
        for u in range(8):
            group, piece = place(24 + u)
            grads[j, piece, group] = jnp.zeros((2, D, D), BF16)
        return carry

    def place(w):
        t = (w + h + 1) % 32
        other = t % 8
        return t // 8, 2 * ((other // 2 + 4 - z) % 4) + (other + x) % 2

    lax.fori_loop(0, HEADS, clear, 0)
    spread_to(0, 10, 11, 2, 4)
    spread_from(0, 6, 7)
    spread_to(0, 9, 1)
    spread_from(0, 3, 5)
    for j in range(2, HEADS):
        for copy in partner_in(j) + local_in(j):
            copy.start()
    spread_to(0, 6, 7)
    spread_from(0, 8)
    first_spread(1)

    starts = (16, 8, jnp.where(case_a, 8, 0))
    lows = (lo_8, lo_b, jnp.where(case_a, lo_8, lo_b))
    sets = (2, 1, jnp.where(case_a, 1, 0))

    def begin(j):
        for copy in local_in(j):
            copy.wait()
        for copy in partner_in(j):
            copy.wait_recv()
        spread_to(j, 3, 5, 8)
        for w in range(3 * SET):
            group, piece = place(w)
            row = pl.ds(w % SET * D, D)
            kb, vb = held[j, piece, group, 0], held[j, piece, group, 1]
            kx[w // SET, row, :] = kb
            vx[w // SET, row, :] = vb
            kt[w // SET, :, row] = kb.T
            vt[w // SET, :, row] = vb.T
        dk[...] = jnp.zeros_like(dk)
        dv[...] = jnp.zeros_like(dv)

    def finish(j):
        for copy in local_out(j) + partner_out(j, mine):
            copy.start()
        for w in range(SET):
            row = pl.ds(w * D, D)
            for n, acc, f in ((0, dk, SCALE), (1, dv, 1.0)):
                for start, value in (
                    (16, acc[0, row, :]),
                    (8, acc[1, row, :] + acc[2, row, :] * sel),
                    (0, acc[2, row, :] * (1.0 - sel)),
                ):
                    group, piece = place(start + w)
                    grads[j, piece, group, n] = (value * f).astype(BF16)
        collect_from(j, 8, 3, 5, 9, 10)

    def add(j, piece, source, groups, count, parts):
        for g in range(count):
            for n in parts:
                total = grads[j, piece, groups.start + g, n].astype(F32)
                for p in source:
                    total = total + sums[j, p, groups.start + g, n].astype(F32)
                grads[j, piece, groups.start + g, n] = total.astype(BF16)

    def collect_far_x(j):
        collect_to(j, 8)
        add(j, FAR, (FAR_X,), COLLECT[8][3], 3, (0, 1))
        collect_from(j, 6, 7)

    def collect_beside(j):
        collect_to(j, 3, 5)
        add(j, BESIDE, (UP_X,), COLLECT[3][3], 3, (0, 1))
        add(j, BESIDE, (DOWN_X,), COLLECT[5][3], 3, (0, 1))
        collect_from(j, 1)

    def collect_far(j):
        collect_to(j, 6, 7)
        add(j, UP, (FAR,), COLLECT[6][3], 3, (0,))
        add(j, DOWN, (FAR,), COLLECT[7][3], 3, (1,))
        collect_from(j, 2, 4)

    def collect_own(j):
        collect_to(j, 1, 2, 4, 9, 10)
        add(j, OWN, (UP, DOWN, BESIDE), every, 4, (0, 1))
        for k in range(2):
            owner_out(j, k).start()
        back(j).start()

    def phases(j, i, s_scr, e_scr, ds_scr):
        lane = pl.ds(pl.multiple_of(i * 2 * D, 2 * D), 2 * D)

        def both(own, other):
            a, b = own[j, :, lane], other[j, :, lane]
            return jnp.where(later, a, b), jnp.where(later, b, a)

        q1, q2 = (jnp.concatenate([a[:, :D], a[:, D:]], axis=0) for a in both(qm, qo))
        g1, g2 = both(gm, go)
        qs = (q1, q2, jnp.where(case_a, q1, q2))
        ms = []
        for t in range(3):
            m = jnp.full((8, 2 * D), -BIG, F32)
            for c in range(4):
                s = nt(kx[sets[t], pl.ds(c * CHUNK, CHUNK), :], qs[t])
                if t < 2 and c == 3:
                    kpos = lax.broadcasted_iota(jnp.int32, (D, 2 * D), 0)
                    qpos = lax.broadcasted_iota(jnp.int32, (D, 2 * D), 1) % D
                    s = jnp.concatenate([s[:D], jnp.where(kpos <= qpos, s[D:], -BIG)], axis=0)
                s_scr[t, pl.ds(c * CHUNK, CHUNK), :] = s
                for b in range(2):
                    bias = jnp.where(starts[t] + 2 * c + b >= lows[t], 0.0, -BIG)
                    part = jnp.max(s[b * D : (b + 1) * D].reshape(16, 8, 2 * D), axis=0)
                    m = jnp.maximum(m, part + bias)
            ms.append(jnp.max(m, axis=0, keepdims=True))
            yield
        m1 = jnp.where(case_a, jnp.maximum(ms[0], ms[2]), ms[0])
        m2 = jnp.where(case_a, ms[1], jnp.maximum(ms[1], ms[2]))
        peaks = (m1, m2, jnp.where(case_a, m1, m2))
        sums, outs = [], []
        factor = SCALE * LOG2E
        for t in range(3):
            l = jnp.zeros((8, 2 * D), F32)
            for c in range(4):
                es = []
                for b in range(2):
                    bias = jnp.where(starts[t] + 2 * c + b >= lows[t], 0.0, BIG)
                    e = jnp.exp2(
                        s_scr[t, pl.ds(c * CHUNK + b * D, D), :] * factor - (peaks[t] * factor + bias)
                    )
                    l = l + jnp.sum(e.reshape(16, 8, 2 * D), axis=0)
                    es.append(e.astype(BF16))
                e_scr[t, pl.ds(c * CHUNK, CHUNK), :] = jnp.concatenate(es, axis=0)
            sums.append(jnp.sum(l, axis=0, keepdims=True))
            outs.append(nn(vt[sets[t]], e_scr[t]))
            yield
        l1 = sums[0] + sums[2] * sel
        l2 = sums[1] + sums[2] * (1.0 - sel)
        o1 = outs[0] + outs[2] * sel
        o2 = outs[1] + outs[2] * (1.0 - sel)
        gs, gts, qps, deltas, results, factors = [], [], [], [], [], []
        for q, g, o, l in ((q1, g1, o1, l1), (q2, g2, o2, l2)):
            inv = 1.0 / l
            half = (o * inv).astype(BF16)
            gt = turned(g)
            deltas.append(jnp.sum(gt.astype(F32) * half.astype(F32), axis=0, keepdims=True))
            gts.append(gt)
            wide = jnp.broadcast_to(inv, (D, 2 * D))
            column = jnp.concatenate([wide[:, :D].T, wide[:, D:].T], axis=0)
            rows = jnp.concatenate([g[:, :D], g[:, D:]], axis=0)
            gs.append((rows.astype(F32) * column).astype(BF16))
            qps.append((q.astype(F32) * column).astype(BF16))
            factors.append(inv * SCALE)
            results.append(turned(half))
        om[j, :, lane] = jnp.where(later, results[0], results[1])
        oo[j, :, lane] = jnp.where(later, results[1], results[0])
        gs.append(jnp.where(case_a, gs[0], gs[1]))
        gts.append(jnp.where(case_a, gts[0], gts[1]))
        qps.append(jnp.where(case_a, qps[0], qps[1]))
        deltas.append(jnp.where(case_a, deltas[0], deltas[1]))
        yield
        dqs = []
        for t in range(3):
            for c in range(2):
                row = pl.ds(c * 2 * CHUNK, 2 * CHUNK)
                dp = nn(vx[sets[t], row, :], gts[t])
                ds_scr[row, :] = (dp - deltas[t]).astype(BF16) * e_scr[t, row, :]
            for c in range(2):
                row = pl.ds(c * 2 * CHUNK, 2 * CHUNK)
                dv[t, row, :] += nn(e_scr[t, row, :], gs[t])
                dk[t, row, :] += nn(ds_scr[row, :], qps[t])
            dqs.append(nn(kt[sets[t]], ds_scr[...]))
            yield
        r1 = turned(((dqs[0] + dqs[2] * sel) * factors[0]).astype(BF16))
        r2 = turned(((dqs[1] + dqs[2] * (1.0 - sel)) * factors[1]).astype(BF16))
        dqm[j, :, lane] = jnp.where(later, r1, r2)
        dqo[j, :, lane] = jnp.where(later, r2, r1)
        yield

    def two_pairs(j, i):
        first = phases(j, 2 * i, s_scr, e_scr, ds_scr)
        second = phases(j, 2 * i + 1, s_scr2, e_scr2, ds_scr2)
        for _ in range(3):
            next(first)
        for _ in range(2):
            for _ in range(3):
                next(first)
                next(second)
            next(first)
        for _ in range(5):
            next(second)

    def step(t, carry):
        j, i = t // STEPS, t % STEPS

        @pl.when(i == 0)
        def _():
            begin(j)

            @pl.when(j < HEADS - 2)
            def _():
                enter(j + 2)

        two_pairs(j, i)

        def service(at, condition, function):
            pl.when(jnp.logical_and(i == at, condition))(function)

        def first_services():
            @pl.when(j < HEADS - 1)
            def _():
                spread_to(j + 1, 10, 11, 2, 4)
                spread_from(j + 1, 6, 7)

            @pl.when(j > 0)
            def _():
                collect_far_x(j - 1)

            @pl.when(j < HEADS - 1)
            def _():
                spread_to(j + 1, 9, 1)
                spread_from(j + 1, 3, 5)

            @pl.when(j > 0)
            def _():
                collect_beside(j - 1)

        def spread_last():
            spread_to(j + 1, 6, 7)
            spread_from(j + 1, 8)

        def spread_first():
            first_spread(j + 2)

        service(0, True, first_services)
        service(1, j < HEADS - 1, spread_last)
        service(1, j > 0, lambda: collect_far(j - 1))
        service(2, j < HEADS - 2, spread_first)
        service(3, j > 0, lambda: collect_own(j - 1))

        @pl.when(i == STEPS - 1)
        def _():
            finish(j)

        return carry

    lax.fori_loop(0, HEADS * STEPS, step, 0)
    def final(j):
        back(j).wait_recv()
        for k in range(2):
            owner_in(j, k).wait_recv()
        for n, out in ((0, dk_out), (1, dv_out)):
            own = grads[j, 0, 2 + core, n].astype(F32)
            other = swapped[j, n].astype(F32)
            first, second = returned[0, j, n].astype(F32), returned[1, j, n].astype(F32)
            low = jnp.where(later, other, own) + first
            high = jnp.where(later, own, other) + second
            out[:, j * D : (j + 1) * D] = low.astype(BF16)
            out[:, (HEADS + j) * D : (HEADS + j + 1) * D] = high.astype(BF16)

    def drain(j, carry):
        swap_out(j).wait_send()
        back(j).wait_send()
        for k in range(2):
            onward_out(j, k).wait_send()
            owner_out(j, k).wait_send()
        for n in range(1, 12):
            spread(n, j).wait_send()
        for n in range(1, 11):
            collect(n, j).wait_send()
        for copy in partner_in(j):
            copy.wait_send()
        for copy in local_out(j):
            copy.wait()
        for copy in partner_out(j, mine):
            copy.wait_send()
        for copy in partner_out(j, theirs):
            copy.wait_recv()
        return carry

    for j in range(HEADS - 1):
        final(j)
    collect_far_x(HEADS - 1)
    collect_beside(HEADS - 1)
    lax.fori_loop(0, HEADS - 1, drain, 0)
    collect_far(HEADS - 1)
    collect_own(HEADS - 1)
    final(HEADS - 1)
    drain(HEADS - 1, 0)


def attend(ids, queries, cotangent, keys, values):
    shape = jax.ShapeDtypeStruct
    anywhere, vmem = pl.BlockSpec(memory_space=pl.ANY), pl.BlockSpec(memory_space=pltpu.VMEM)
    blocks = pltpu.VMEM((HEADS, 8, 4, 2, D, D), BF16)
    wide = pltpu.VMEM((HEADS, D, GRP * D), BF16)
    sem = pltpu.SemaphoreType.DMA
    return pl.pallas_call(
        kernel,
        in_specs=[pl.BlockSpec(memory_space=pltpu.SMEM), anywhere, anywhere, vmem, vmem],
        out_specs=[anywhere, anywhere, vmem, vmem],
        out_shape=[shape(queries.shape, BF16)] * 2 + [shape(keys.shape, BF16)] * 2,
        scratch_shapes=[
            pltpu.VMEM((2 * HEADS, 2, D, D), BF16),
            blocks,
            blocks,
            blocks,
            pltpu.VMEM((2, HEADS, 2, D, D), BF16),
            pltpu.VMEM((HEADS, 2, D, D), BF16),
        ]
        + [wide] * 8
        + [
            pltpu.VMEM((3, SET * D, D), BF16),
            pltpu.VMEM((3, SET * D, D), BF16),
            pltpu.VMEM((3, D, SET * D), BF16),
            pltpu.VMEM((3, D, SET * D), BF16),
            pltpu.VMEM((3, SET * D, 2 * D), F32),
            pltpu.VMEM((3, SET * D, 2 * D), BF16),
            pltpu.VMEM((SET * D, 2 * D), BF16),
            pltpu.VMEM((3, SET * D, 2 * D), F32),
            pltpu.VMEM((3, SET * D, 2 * D), BF16),
            pltpu.VMEM((SET * D, 2 * D), BF16),
            pltpu.VMEM((3, SET * D, D), F32),
            pltpu.VMEM((3, SET * D, D), F32),
        ]
        + [sem((HEADS,))] * 2
        + [sem((2, HEADS))] * 2
        + [sem((11, HEADS))] * 2
        + [sem((10, HEADS))] * 2
        + [sem((2, HEADS))] * 2
        + [sem((HEADS,))] * 2
        + [sem((2, HEADS))] * 6,
        compiler_params=pltpu.CompilerParams(
            collective_id=0, has_side_effects=True, vmem_limit_bytes=62 * 1024 * 1024
        ),
        cost_estimate=pl.CostEstimate(
            flops=HEADS * 24 * GRP * 24 * D**3, bytes_accessed=16 * 1024 * 1024, transcendentals=0
        ),
    )(ids, queries, cotangent, keys, values)


def body(queries, keys, values, cotangent, doc_ids):
    attended, grad_query, key_gradient, value_gradient = attend(
        doc_ids, queries, cotangent, keys, values
    )
    return attended, grad_query, key_gradient, value_gradient


def solution(mesh):
    rows = P(("ctx", "head"), None)
    return jax.shard_map(
        body,
        mesh=mesh,
        in_specs=(rows, rows, rows, rows, P()),
        out_specs=(rows, rows, rows, rows),
        check_vma=False,
    )
```
